256 devices in a mesh: ctx: 16 (over x_hi, z), head: 8 (over x_lo, y), rep: 2 (over core).
Axes of the slice: x: 4 (x_hi: 2, x_lo: 2; x = x_hi * 2 + x_lo), y: 4, z: 8, core: 2. Of those that a mesh axis runs over, the one named last changes fastest.
Arguments:
- q_new: bfloat16 [4096, 16384], P(('rep', 'ctx'), 'head'), parts along dimension 0, may hold values from -32 to 32
- k_new: bfloat16 [4096, 1024], P(('rep', 'ctx'), 'head'), parts along dimension 0, may hold values from -6 to 6
- v_new: bfloat16 [4096, 1024], P(('rep', 'ctx'), 'head'), parts along dimension 0, may hold values from -6 to 6
- k_cache: bfloat16 [20480, 1024], P(('rep', 'ctx'), 'head'), parts along dimension 0, may hold values from -32 to 32
- v_cache: bfloat16 [20480, 1024], P(('rep', 'ctx'), 'head'), parts along dimension 0, may hold values from -6 to 6
- new_pos: int32 [4096], P(('rep', 'ctx')), parts along dimension 0, may hold values from 10240 to 12287, as said below
Outputs:
- attended: bfloat16 [4096, 16384], P(('rep', 'ctx'), 'head'), parts along dimension 0
The draws below stay inside these ranges and needn't reach their ends.
There are 2 independent parts, one for each index of `rep`. The reference program is written for one: setup_inputs(seed, part) draws one part's arguments, and reference() takes and returns one part's arrays. A program takes and returns all parts, laid end to end along the dimension named above; each array names one. Nothing has to cross between parts.
Inputs may be any that keep to these rules, and one draw needn't show every extreme that they name: `new_pos`: the new tokens form 2 * 16 blocks of 64 consecutive positions; index d of ctx holds block c and block 31 - c, in this order, for a c that a permutation drawn per request gives; all new positions are 10240 .. 12287, each once.
All inputs are finite; a program needn't handle non-finite values.
Results may differ from the reference program's by a relative error of at most 0.012.
Values may be sent and summed in bfloat16 or wider, within the bound.
A program may use at most 128 MiB of HBM per device.

```python
import jax
import jax.numpy as jnp
from jax import lax

HQ = 128
KVH = 8
DH = 128
C_DEV = 640
Q_DEV = 128
CTX = 10240
NEW = 2048
N_CTX = 16


def draw_q_new(key, part):
    key = jax.random.fold_in(key, 11)
    sample = jnp.clip(jax.random.normal(key, (NEW, HQ * DH), jnp.float32), -6.0, 6.0)
    return sample.astype(jnp.bfloat16)


def draw_k_cache(key, part):
    key = jax.random.fold_in(key, 12)
    sample = jnp.clip(jax.random.normal(key, (CTX, KVH * DH), jnp.float32), -6.0, 6.0)
    return sample.astype(jnp.bfloat16)


def draw_new_pos(key, part):
    key = jax.random.fold_in(key, 13)
    order = jax.random.permutation(key, N_CTX).astype(jnp.int32)
    half = Q_DEV // 2
    offsets = jnp.arange(half, dtype=jnp.int32)
    first = order[:, None] * half + offsets[None, :]
    second = (2 * N_CTX - 1 - order)[:, None] * half + offsets[None, :]
    return (CTX + jnp.concatenate([first, second], axis=1).reshape(-1)).astype(jnp.int32)


def level_of(key, extent, pieces, low, largest):
    def one(dim, shards_of):
        steps = jax.random.uniform(jax.random.fold_in(jax.random.fold_in(key, 6), dim), (shards_of,), jnp.float32, low / len(pieces), largest / len(pieces))
        return jnp.repeat(jnp.exp(steps), extent[dim] // shards_of).reshape((-1,) + (1,) * (len(extent) - dim - 1))

    gain = one(*pieces[0])
    for cut in pieces[1:]:
        gain = gain * one(*cut)
    return gain


def bell_draw(rng, shape, scale, limit, cuts=(), held_as=jnp.bfloat16):
    result = scale * jax.random.normal(rng, shape, jnp.float32)
    if cuts:
        result = result * level_of(rng, shape, cuts, -0.22, 0.18)
    return jnp.clip(result, -limit, limit).astype(held_as)


def setup_inputs(seed: int = 0, part: int = 0) -> dict:
    streams_of = jax.random.split(jax.random.key(seed), 7)
    part_splits = jax.random.split(jax.random.fold_in(streams_of[6], part), 7)
    q_new = draw_q_new(jax.random.fold_in(jax.random.fold_in(streams_of[6], part), 71), part)
    k_new = bell_draw(part_splits[1], (NEW, KVH * DH), 1.0, 6.0, ((0, 16), (1, 8)))
    v_new = bell_draw(part_splits[2], (NEW, KVH * DH), 1.0, 6.0, ((0, 16), (1, 8)))
    k_cache = draw_k_cache(jax.random.fold_in(jax.random.fold_in(streams_of[6], part), 71), part)
    v_cache = bell_draw(part_splits[4], (CTX, KVH * DH), 1.0, 6.0, ((0, 16), (1, 8)))
    new_pos = draw_new_pos(jax.random.fold_in(jax.random.fold_in(streams_of[6], part), 71), part)
    return dict(q_new=q_new, k_new=k_new, v_new=v_new, k_cache=k_cache, v_cache=v_cache, new_pos=new_pos)


def rotate(values_in, positions):
    rows = values_in.shape[0]
    heads = values_in.shape[1] // DH
    half = DH // 2
    grid = values_in.astype(jnp.float32).reshape(rows, heads, DH)
    freqs = 500000.0 ** (-(2.0 * jnp.arange(half, dtype=jnp.float32)) / DH)
    angles = positions.astype(jnp.float32)[:, None] * freqs[None, :]
    cosine = jnp.cos(angles)[:, None, :]
    sine = jnp.sin(angles)[:, None, :]
    lower = grid[..., :half]
    upper = grid[..., half:]
    turned = jnp.concatenate([lower * cosine - upper * sine, upper * cosine + lower * sine], axis=-1)
    return turned.reshape(rows, heads * DH).astype(jnp.bfloat16)


def attend_block(queries, query_pos, keys, values, key_pos):
    qrows = queries.shape[0]
    krows = keys.shape[0]
    kv_heads = keys.shape[1] // DH
    q_heads = queries.shape[1] // DH
    group = q_heads // kv_heads
    query_heads = queries.reshape(qrows, kv_heads, group, DH).astype(jnp.float32)
    key_heads = keys.reshape(krows, kv_heads, DH).astype(jnp.float32)
    value_heads = values.reshape(krows, kv_heads, DH).astype(jnp.float32)
    scores = jnp.einsum("qkgd,nkd->kgqn", query_heads, key_heads) * (1.0 / (DH ** 0.5))
    allowed = key_pos[None, :] <= query_pos[:, None]
    scores = jnp.where(allowed[None, None], scores, jnp.float32(-1e30))
    top = jnp.max(scores, axis=-1)
    expo = jnp.exp(scores - top[..., None])
    total = jnp.sum(expo, axis=-1)
    weights = expo.astype(jnp.bfloat16).astype(jnp.float32)
    mixed = jnp.einsum("kgqn,nkd->qkgd", weights, value_heads)
    mixed = mixed / jnp.transpose(total, (2, 0, 1))[..., None]
    part_out = mixed.reshape(qrows, q_heads * DH).astype(jnp.bfloat16)
    part_lse = jnp.transpose(top + jnp.log(total), (2, 0, 1)).reshape(qrows, q_heads)
    return part_out, part_lse


def combine_partials(outs, lses):
    shards, qrows, heads = lses.shape
    top = jnp.max(lses, axis=0)
    total = top + jnp.log(jnp.sum(jnp.exp(lses - top[None]), axis=0))
    weights = jnp.exp(lses - total[None])
    spread = outs.astype(jnp.float32).reshape(shards, qrows, heads, DH)
    summed = jnp.sum(weights[..., None] * spread, axis=0)
    return summed.reshape(qrows, heads * DH).astype(jnp.bfloat16)


def reference(q_new, k_new, v_new, k_cache, v_cache, new_pos):
    width = KVH * DH
    q_rot = rotate(q_new, new_pos)
    k_rot = rotate(k_new, new_pos)
    keys_all = jnp.concatenate([k_cache.reshape(N_CTX, C_DEV, width), k_rot.reshape(N_CTX, Q_DEV, width)], axis=1)
    values_all = jnp.concatenate([v_cache.reshape(N_CTX, C_DEV, width), v_new.reshape(N_CTX, Q_DEV, width)], axis=1)
    cache_pos = jnp.arange(CTX, dtype=jnp.int32).reshape(N_CTX, C_DEV)
    pos_all = jnp.concatenate([cache_pos, new_pos.astype(jnp.int32).reshape(N_CTX, Q_DEV)], axis=1)

    def one_block(block_in):
        queries, query_pos = block_in

        def one_shard(shard_in):
            keys, values, key_pos = shard_in
            return attend_block(queries, query_pos, keys, values, key_pos)

        outs, lses = lax.map(one_shard, (keys_all, values_all, pos_all))
        return combine_partials(outs, lses)

    blocks = lax.map(one_block, (q_rot.reshape(N_CTX, Q_DEV, HQ * DH), new_pos.astype(jnp.int32).reshape(N_CTX, Q_DEV)))
    return blocks.reshape(NEW, HQ * DH)
```

```python
import functools
import math

import jax
import jax.numpy as jnp
import numpy as np
from jax import lax
from jax.experimental import pallas as pl
from jax.experimental.pallas import tpu as pltpu
from jax.sharding import PartitionSpec as P

DH = 128
HALF = 64
F32 = jnp.float32
BF16 = jnp.bfloat16
MESH = pl.DeviceIdType.MESH
LOG2E = math.log2(math.e)
SCALE = LOG2E / math.sqrt(DH)
NEG = -1e30
CACHED = 10240

ZN = 8
PART = 384
OLD = 320
ROWS = 2 * PART + 16
QB = 512
NQB = 4
CB = 1024
NCB = 2
OROWS = DH + 16
EARLY = 3
UNITS = 2 * ZN


def mm(a, b):
    return lax.dot_general(
        a, b, (((1,), (0,)), ((), ())), preferred_element_type=F32
    )


def turn(x, cosine, sine):
    lower, upper = x[:HALF], x[HALF:]
    return jnp.concatenate(
        [lower * cosine - upper * sine, upper * cosine + lower * sine], axis=0
    )


def kernel(
    ny, q_ref, kn_ref, vn_ref, kc_ref, vc_ref, pos_ref, freq_ref, out_ref,
    qt, fq, kv, qp, acc, top, s0, s1, x0, x1, so, fo, ro,
    kv_send, kv_recv, q1_send, q1_recv, q2_send, q2_recv,
    o1_send, o1_recv, o2_send, o2_recv, p_send, p_recv,
):
    ctx = lax.axis_index("ctx")
    head = lax.axis_index("head")
    hi, z = ctx // ZN, ctx % ZN
    lo, y = head // ny, head % ny
    right = {"ctx": hi * ZN + (z + 1) % ZN, "head": head}
    left = {"ctx": hi * ZN + (z + ZN - 1) % ZN, "head": head}
    side_a = {"ctx": ctx, "head": (1 - lo) * ny + y}
    side_b = {"ctx": (1 - hi) * ZN + z, "head": (1 - lo) * ny + y}
    partner = {"ctx": (1 - hi) * ZN + z, "head": head}
    everyone = (right, left, side_a, side_b, partner)

    barrier = pltpu.get_barrier_semaphore()
    for other in everyone:
        pl.semaphore_signal(barrier, inc=1, device_id=other, device_id_type=MESH)

    def remote(src, dst, send, recv, target):
        return pltpu.make_async_remote_copy(
            src_ref=src, dst_ref=dst, send_sem=send, recv_sem=recv,
            device_id=target, device_id_type=MESH,
        )

    def kv_copy(d, s):
        if s <= 2:
            src = kv.at[0, (s - 1) if d == 0 else (2 - s)]
        else:
            src = kv.at[s - 2, d]
        return remote(
            src, kv.at[s, d], kv_send.at[d, s - 1], kv_recv.at[d, s - 1],
            right if d == 0 else left,
        )

    def q_first(b):
        return remote(
            qt.at[0, b], fq.at[b], q1_send.at[b], q1_recv.at[b],
            side_a if b % 2 == 0 else side_b,
        )

    def q_second(b):
        return remote(
            fq.at[b], qt.at[1, b], q2_send.at[b], q2_recv.at[b],
            side_b if b % 2 == 0 else side_a,
        )

    def o_first(b):
        return remote(
            so.at[b], fo.at[b], o1_send.at[b], o1_recv.at[b],
            side_a if b % 2 == 0 else side_b,
        )

    def o_second(b):
        return remote(
            fo.at[b], ro.at[b], o2_send.at[b], o2_recv.at[b],
            side_b if b % 2 == 0 else side_a,
        )

    p_copy = remote(qp.at[0], qp.at[1], p_send, p_recv, partner)

    relative = pos_ref[...].astype(F32) - CACHED
    angle = freq_ref[...] * pos_ref[...].astype(F32)
    cosine, sine = jnp.cos(angle), jnp.sin(angle)
    k_rot = turn(kn_ref[...].astype(F32).T, cosine, sine).T.astype(BF16)
    for d in range(2):
        kv[0, d, 0:OLD, :] = kc_ref[d * OLD:(d + 1) * OLD, :]
        kv[0, d, OLD:PART, :] = k_rot[d * HALF:(d + 1) * HALF]
        v = jnp.concatenate(
            [vc_ref[d * OLD:(d + 1) * OLD, :], vn_ref[d * HALF:(d + 1) * HALF, :]], axis=0
        ).astype(F32)
        for t in range(3):
            kv[0, d, PART + DH * t:PART + DH * (t + 1), :] = (
                v[DH * t:DH * (t + 1)].T.astype(BF16)
            )
        number = relative[:, d * HALF:d * HALF + 1] * (1.0 / HALF)
        kv[0, d, 2 * PART:ROWS, :] = jnp.broadcast_to(number, (16, DH)).astype(BF16)
    qp[0] = jnp.broadcast_to(relative, (8, DH))

    pl.semaphore_wait(barrier, len(everyone))
    for s in (1, 2):
        for d in range(2):
            kv_copy(d, s).start()
    p_copy.start()
    for b in range(NQB):
        for h in range(QB // DH):
            c = b * QB + h * DH
            x = q_ref[:, c:c + DH].astype(F32).T
            qt[0, b, :, h * DH:(h + 1) * DH] = turn(x, cosine, sine).astype(BF16)
        q_first(b).start()
    acc[...] = jnp.zeros(acc.shape, F32)
    top[...] = jnp.full(top.shape, NEG, F32)

    def unit(u):
        group = jnp.where((u >= EARLY) & (u < EARLY + ZN), 1, 0)
        step = jnp.where(u < EARLY, u, jnp.where(u < EARLY + ZN, u - EARLY, u - ZN))
        return group, step

    def score(u, blk, s_ref, x_ref):
        group, step = unit(u)
        q = jnp.concatenate([qt[group, 2 * blk], qt[group, 2 * blk + 1]], axis=1)
        qpos = qp[group][0:1]
        best = None
        for d in range(2):
            s = mm(kv[step, d, 0:PART, :], q) * SCALE
            number = kv[step, d, 2 * PART:ROWS, :].astype(F32)[0:1]
            kpos = number * HALF + lax.broadcasted_iota(jnp.int32, (HALF, DH), 0).astype(F32)
            bias = jnp.where(kpos <= qpos, 0.0, NEG)
            fresh = s[OLD:] + jnp.concatenate([bias] * (CB // DH), axis=1)
            s_ref[d * PART:d * PART + OLD, :] = s[:OLD]
            s_ref[d * PART + OLD:(d + 1) * PART, :] = fresh
            m = jnp.maximum(
                jnp.max(s[:OLD], axis=0, keepdims=True),
                jnp.max(fresh, axis=0, keepdims=True),
            )
            best = m if best is None else jnp.maximum(best, m)
        x_ref[...] = best

    def mix(u, blk, s_ref, x_ref):
        group, step = unit(u)
        before = top[group, blk]
        after = jnp.maximum(before, x_ref[...])
        top[group, blk] = after
        fade = jnp.exp2(before - after)
        p = jnp.exp2(s_ref[...] - after).astype(BF16)
        v = jnp.concatenate(
            [
                kv[step, d, PART + DH * t:PART + DH * (t + 1), :]
                for d in range(2) for t in range(3)
            ],
            axis=1,
        )
        v = jnp.concatenate([v, jnp.ones((16, 2 * PART), BF16)], axis=0)
        acc[group, blk] = acc[group, blk] * fade + mm(v, p)

    def kv_arrive(s):
        for d in range(2):
            kv_copy(d, s).wait_recv()
            if s + 2 < ZN:
                kv_copy(d, s + 2).start()

    def q_pass(b):
        q_first(b).wait_recv()
        q_second(b).start()

    def o_pass(b):
        o_first(b).wait_recv()
        o_second(b).start()

    def partials(group, b):
        blk, c = b // 2, (b % 2) * QB
        a = acc[group, blk, :, c:c + QB]
        total = a[DH:DH + 1]
        lse = top[group, blk, :, c:c + QB] + jnp.log(total) * LOG2E
        return a[:DH] / total, lse

    def after_first(u):
        @pl.when(u == 0)
        def _():
            kv_arrive(1)
            q_pass(0)
            q_pass(1)

        @pl.when(u == 1)
        def _():
            kv_arrive(2)
            q_pass(2)
            q_pass(3)

        @pl.when(u == 2)
        def _():
            p_copy.wait_recv()
            for b in range(NQB):
                q_second(b).wait_recv()

        for at, s in ((3, 3), (4, 4), (6, 5), (8, 6), (9, 7)):
            @pl.when(u == at)
            def _(s=s):
                kv_arrive(s)

        for at, b in ((12, 0), (13, 2)):
            @pl.when(u == at)
            def _(b=b):
                o_pass(b)
                o_pass(b + 1)

    score(0, 0, s0, x0)

    def body(u, carry):
        score(u, 1, s1, x1)
        mix(u, 0, s0, x0)
        after_first(u)
        score(jnp.minimum(u + 1, UNITS - 1), 0, s0, x0)
        mix(u, 1, s1, x1)

        @pl.when(u == EARLY + ZN - 1)
        def _():
            for b in range(NQB):
                o, lse = partials(1, b)
                so[b, 0:DH, :] = o.astype(BF16)
                high = lse.astype(BF16).astype(F32)
                middle = (lse - high).astype(BF16).astype(F32)
                low = lse - high - middle
                row = lax.broadcasted_iota(jnp.int32, (16, QB), 0)
                so[b, DH:OROWS, :] = jnp.where(
                    row == 0, high, jnp.where(row == 1, middle, low)
                ).astype(BF16)
                o_first(b).start()

        return carry

    lax.fori_loop(0, UNITS, body, 0)

    for b in range(NQB):
        o_second(b).wait_recv()
        own, lse = partials(0, b)
        other = ro[b, 0:DH, :].astype(F32)
        rows = ro[b, DH:OROWS, :].astype(F32)
        lse_other = rows[0:1] + rows[1:2] + rows[2:3]
        largest = jnp.maximum(lse, lse_other)
        e_own, e_other = jnp.exp2(lse - largest), jnp.exp2(lse_other - largest)
        share = 1.0 / (e_own + e_other)
        result = own * (e_own * share) + other * (e_other * share)
        for h in range(QB // DH):
            c = b * QB + h * DH
            out_ref[:, c:c + DH] = result[:, h * DH:(h + 1) * DH].T.astype(BF16)

    for d in range(2):
        for s in range(1, ZN):
            kv_copy(d, s).wait_send()
    p_copy.wait_send()
    for b in range(NQB):
        q_first(b).wait_send()
        q_second(b).wait_send()
        o_first(b).wait_send()
        o_second(b).wait_send()


def solution(mesh):
    ny = mesh.shape["head"] // 2
    freqs = 500000.0 ** (-(2.0 * np.arange(HALF, dtype=np.float64)) / DH)
    freqs = np.broadcast_to(freqs.astype(np.float32)[:, None], (HALF, DH))

    def part(q_new, k_new, v_new, k_cache, v_cache, new_pos):
        dma = pltpu.SemaphoreType.DMA
        return pl.pallas_call(
            functools.partial(kernel, ny),
            out_shape=jax.ShapeDtypeStruct(q_new.shape, BF16),
            in_specs=[pl.BlockSpec(memory_space=pltpu.VMEM)] * 7,
            out_specs=pl.BlockSpec(memory_space=pltpu.VMEM),
            scratch_shapes=[
                pltpu.VMEM((2, NQB, DH, QB), BF16),
                pltpu.VMEM((NQB, DH, QB), BF16),
                pltpu.VMEM((ZN, 2, ROWS, DH), BF16),
                pltpu.VMEM((2, 8, DH), F32),
                pltpu.VMEM((2, NCB, OROWS, CB), F32),
                pltpu.VMEM((2, NCB, 1, CB), F32),
                pltpu.VMEM((2 * PART, CB), F32),
                pltpu.VMEM((2 * PART, CB), F32),
                pltpu.VMEM((1, CB), F32),
                pltpu.VMEM((1, CB), F32),
                pltpu.VMEM((NQB, OROWS, QB), BF16),
                pltpu.VMEM((NQB, OROWS, QB), BF16),
                pltpu.VMEM((NQB, OROWS, QB), BF16),
                dma((2, ZN - 1)), dma((2, ZN - 1)),
                dma((NQB,)), dma((NQB,)), dma((NQB,)), dma((NQB,)),
                dma((NQB,)), dma((NQB,)), dma((NQB,)), dma((NQB,)),
                dma, dma,
            ],
            compiler_params=pltpu.CompilerParams(
                collective_id=0, has_side_effects=True, vmem_limit_bytes=48 << 20
            ),
        )(q_new, k_new, v_new, k_cache, v_cache, new_pos.reshape(1, -1), jnp.asarray(freqs))

    rows = P(("rep", "ctx"), "head")
    return jax.shard_map(
        part,
        mesh=mesh,
        in_specs=(rows,) * 5 + (P(("rep", "ctx")),),
        out_specs=rows,
        check_vma=False,
    )
```

```python
import math

import jax
import jax.numpy as jnp
import numpy as np
from jax import lax
from jax.experimental import pallas as pl
from jax.experimental.pallas import tpu as pltpu
from jax.sharding import PartitionSpec as P

DH = 128
HALF = 64
F32 = jnp.float32
BF16 = jnp.bfloat16
MESH = pl.DeviceIdType.MESH
LOG2E = math.log2(math.e)
SCALE = LOG2E / math.sqrt(DH)
NEG = -1e30
CACHED = 10240
Q_ROWS = 128

ZN = 8
SIZES = (384, 256)
OLD = 640
NEW = 128
QB = 512
NQB = 4
CB = 1024
NCB = 2
ROWS = 2 * NEW + 16
OROWS = DH + 16
OWN, OTHER = 0, 1
UNITS = (
    [(OWN, b, s) for s in (0, 1) for b in (0, 1)]
    + [(OTHER, 0, 0), (OTHER, 0, 1), (OWN, 0, 2), (OWN, 1, 2), (OTHER, 0, 2)]
    + [(OWN, 0, 3), (OWN, 1, 3), (OTHER, 0, 3)]
    + [(OTHER, 1, s) for s in range(4)]
    + [(OTHER, b, s) for s in (4, 5) for b in (0, 1)]
    + [(OWN, b, 4) for b in (0, 1)]
    + [(OTHER, b, s) for s in (6, 7) for b in (0, 1)]
    + [(OWN, b, s) for s in (5, 6, 7) for b in (0, 1)]
)
GROUP = 4
LATE = 2 * ZN // GROUP


def mm(a, b):
    return lax.dot_general(
        a, b, (((1,), (0,)), ((), ())), preferred_element_type=F32
    )


def turn(x, cosine, sine):
    lower, upper = x[:HALF], x[HALF:]
    return jnp.concatenate(
        [lower * cosine - upper * sine, upper * cosine + lower * sine], axis=0
    )


def kernel(
    q_hbm, kn_hbm, vn_hbm, kc_hbm, vc_hbm, pos_hbm, freq_hbm, out_ref,
    q_ref, kn_ref, vn_ref, vc_ref, pos_ref, freq_ref, load_sem,
    qt, kva, kvb, nw, qp, acc, top, s0, s1, x0, x1, so, ro,
    kv_send, kv_recv, n_send, n_recv, q_send, q_recv, o_send, o_recv, w_send, w_recv,
):
    ctx = lax.axis_index("ctx")
    head = lax.axis_index("head")
    hi, z = ctx // ZN, ctx % ZN
    right = {"ctx": hi * ZN + (z + 1) % ZN, "head": head}
    left = {"ctx": hi * ZN + (z + ZN - 1) % ZN, "head": head}
    partner = {"ctx": (1 - hi) * ZN + z, "head": head}
    everyone = (right, left, partner)

    barrier = pltpu.get_barrier_semaphore()
    for other in everyone:
        pl.semaphore_signal(barrier, inc=1, device_id=other, device_id_type=MESH)

    def load(src, dst, i):
        return pltpu.make_async_copy(src, dst, load_sem.at[i])

    vc_load = load(vc_hbm, vc_ref, 0)
    kc_loads = [
        load(kc_hbm.at[pl.ds(0, SIZES[0])], kva.at[0, pl.ds(0, SIZES[0])], 1),
        load(kc_hbm.at[pl.ds(SIZES[0], SIZES[1])], kvb.at[0, pl.ds(0, SIZES[1])], 2),
    ]
    pos_load = load(pos_hbm, pos_ref, 3)
    freq_load = load(freq_hbm, freq_ref, 4)
    kn_load = load(kn_hbm, kn_ref, 5)
    vn_load = load(vn_hbm, vn_ref, 6)
    q_loads = [
        load(q_hbm.at[:, pl.ds(b * QB, QB)], q_ref.at[:, pl.ds(b * QB, QB)], 7 + b)
        for b in range(NQB)
    ]
    for one in (vc_load, *kc_loads, pos_load, freq_load, *q_loads, kn_load, vn_load):
        one.start()

    def remote(src, dst, send, recv, target):
        return pltpu.make_async_remote_copy(
            src_ref=src, dst_ref=dst, send_sem=send, recv_sem=recv,
            device_id=target, device_id_type=MESH,
        )

    def kv_copy(d, s):
        held = kva if s % 2 == 1 - d else kvb
        return remote(
            held.at[max(s - 2, 0)], held.at[s], kv_send.at[d, s - 1], kv_recv.at[d, s - 1],
            right if d == 0 else left,
        )

    def new_at(d, n):
        return 2 * n + d

    def n_copy(d, n):
        src = (n - 1 if d == 0 else 2 - n) if n <= 2 else new_at(d, n - 2)
        return remote(
            nw.at[src], nw.at[new_at(d, n)], n_send.at[d, n - 1], n_recv.at[d, n - 1],
            right if d == 0 else left,
        )

    def q_copy(b):
        return remote(qt.at[0, b], qt.at[1, b], q_send.at[b], q_recv.at[b], partner)

    def o_copy(b):
        return remote(so.at[b], ro.at[b], o_send.at[b], o_recv.at[b], partner)

    w_copy = remote(nw.at[0], nw.at[1], w_send, w_recv, partner)

    vc_load.wait()
    for t in range(3):
        kva[0, SIZES[0] + DH * t:SIZES[0] + DH * (t + 1), :] = (
            vc_ref[DH * t:DH * (t + 1), :].astype(F32).T.astype(BF16)
        )
    for t in range(2):
        r = SIZES[0] + DH * t
        kvb[0, SIZES[1] + DH * t:SIZES[1] + DH * (t + 1), :] = (
            vc_ref[r:r + DH, :].astype(F32).T.astype(BF16)
        )
    for one in kc_loads:
        one.wait()
    pl.semaphore_wait(barrier, len(everyone))
    for s in (1, 2):
        for d in range(2):
            kv_copy(d, s).start()

    pos_load.wait()
    freq_load.wait()
    positions = pos_ref[...].astype(F32)
    relative = positions - CACHED
    angle = freq_ref[:, 0:1] * positions
    cosine, sine = jnp.cos(angle), jnp.sin(angle)
    for b in range(NQB):
        q_loads[b].wait()
        for h in range(QB // DH):
            c = b * QB + h * DH
            x = q_ref[:, c:c + DH].astype(F32).T
            qt[0, b, :, h * DH:(h + 1) * DH] = turn(x, cosine, sine).astype(BF16)
        q_copy(b).start()
    acc[...] = jnp.zeros(acc.shape, F32)
    top[...] = jnp.full(top.shape, NEG, F32)
    qp[...] = jnp.broadcast_to(relative, (8, DH))
    kn_load.wait()
    vn_load.wait()
    nw[0, 0:NEW, :] = turn(kn_ref[...].astype(F32).T, cosine, sine).T.astype(BF16)
    nw[0, NEW:2 * NEW, :] = vn_ref[...].astype(F32).T.astype(BF16)
    number = [
        jnp.broadcast_to(relative[:, d * HALF:d * HALF + 1] * (1.0 / HALF), (8, DH))
        for d in range(2)
    ]
    nw[0, 2 * NEW:ROWS, :] = jnp.concatenate(number, axis=0).astype(BF16)

    def unit(u):
        found = []
        for field in zip(*UNITS):
            value = jnp.int32(field[0])
            for at in range(1, len(field)):
                if field[at] != field[at - 1]:
                    value = jnp.where(u >= at, field[at], value)
            found.append(value)
        return tuple(found)

    def queries(group, blk):
        return jnp.concatenate([qt[group, 2 * blk], qt[group, 2 * blk + 1]], axis=1)

    def score(at, s_ref, x_ref):
        group, blk, step = at
        q = queries(group, blk)
        sa = mm(kva[step, 0:SIZES[0], :], q) * SCALE
        sb = mm(kvb[step, 0:SIZES[1], :], q) * SCALE
        s_ref[0:SIZES[0], :] = sa
        s_ref[SIZES[0]:OLD, :] = sb
        x_ref[...] = jnp.maximum(
            jnp.max(sa, axis=0, keepdims=True), jnp.max(sb, axis=0, keepdims=True)
        )

    def score_new(i, blk, s_ref, x_ref):
        q = queries(0, blk)
        qpos = qp[0:1]
        best = None
        for j in range(GROUP):
            s = mm(nw[i * GROUP + j, 0:NEW, :], q) * SCALE
            number = nw[i * GROUP + j, 2 * NEW:ROWS, :].astype(F32)
            row = lax.broadcasted_iota(jnp.int32, (HALF, DH), 0).astype(F32)
            bias = jnp.concatenate(
                [
                    jnp.where(number[8 * d:8 * d + 1] * HALF + row <= qpos, 0.0, NEG)
                    for d in range(2)
                ],
                axis=0,
            )
            s = s + jnp.concatenate([bias] * (CB // DH), axis=1)
            s_ref[j * NEW:(j + 1) * NEW, :] = s
            m = jnp.max(s, axis=0, keepdims=True)
            best = m if best is None else jnp.maximum(best, m)
        x_ref[...] = best

    def mix_in(group, blk, s, x_ref, tiles):
        before = top[group, blk]
        after = jnp.maximum(before, x_ref[...])
        top[group, blk] = after
        fade = jnp.exp2(before - after)
        p = jnp.exp2(s - after).astype(BF16)
        v = jnp.concatenate(tiles, axis=1)
        v = jnp.concatenate([v, jnp.ones((16, v.shape[1]), BF16)], axis=0)
        acc[group, blk] = acc[group, blk] * fade + mm(v, p)

    def mix(at, s_ref, x_ref):
        group, blk, step = at
        tiles = [
            held[step, size + DH * t:size + DH * (t + 1), :]
            for held, size in ((kva, SIZES[0]), (kvb, SIZES[1]))
            for t in range(size // DH)
        ]
        mix_in(group, blk, s_ref[0:OLD, :], x_ref, tiles)

    def mix_new(i, blk, s_ref, x_ref):
        tiles = [nw[i * GROUP + j, NEW:2 * NEW, :] for j in range(GROUP)]
        mix_in(0, blk, s_ref[0:GROUP * NEW, :], x_ref, tiles)

    def kv_arrive(s):
        for d in range(2):
            kv_copy(d, s).wait_recv()
            if s + 2 < ZN:
                kv_copy(d, s + 2).start()

    def n_arrive(n):
        for d in range(2):
            n_copy(d, n).wait_recv()
            if n + 2 < ZN:
                n_copy(d, n + 2).start()

    def partials(group, b):
        blk, c = b // 2, (b % 2) * QB
        a = acc[group, blk, :, c:c + QB]
        total = a[DH:DH + 1]
        lse = top[group, blk, :, c:c + QB] + jnp.log(total) * LOG2E
        return a[:DH] / total, lse

    def finish(b):
        o, lse = partials(1, b)
        so[b, 0:DH, :] = o.astype(BF16)
        high = lse.astype(BF16).astype(F32)
        middle = (lse - high).astype(BF16).astype(F32)
        low = lse - high - middle
        row = lax.broadcasted_iota(jnp.int32, (16, QB), 0)
        so[b, DH:OROWS, :] = jnp.where(
            row == 0, high, jnp.where(row == 1, middle, low)
        ).astype(BF16)
        o_copy(b).start()

    def q_arrive(b):
        q_copy(b).wait_recv()

    def w_begin():
        w_copy.start()

    def n_begin():
        w_copy.wait_recv()
        for n in (1, 2):
            for d in range(2):
                n_copy(d, n).start()

    after = {
        0: [(kv_arrive, 1)],
        2: [(q_arrive, 0), (q_arrive, 1)],
        4: [(kv_arrive, 2)],
        7: [(kv_arrive, 3)],
        10: [(q_arrive, 2), (q_arrive, 3), (w_begin,)],
        11: [(kv_arrive, 4)],
        15: [(kv_arrive, 5), (n_begin,)],
        19: [(kv_arrive, 6)],
        22: [(kv_arrive, 7)],
        24: [(finish, 0), (finish, 1), (n_arrive, 1)],
        25: [(finish, 2), (finish, 3)],
        26: [(n_arrive, 2)],
        27: [(n_arrive, 3)],
        29: [(n_arrive, 4)],
    }

    def sync(u, odd):
        for at, actions in after.items():
            if at % 2 == odd:
                @pl.when(u == at)
                def _(actions=actions):
                    for action, *given in actions:
                        action(*given)

    score(UNITS[0], s0, x0)

    def body(i, now):
        u = 2 * i
        then = unit(u + 1)
        score(then, s1, x1)
        mix(now, s0, x0)
        sync(u, 0)
        now = unit(u + 2)
        score(now, s0, x0)
        mix(then, s1, x1)
        sync(u + 1, 1)
        return now

    first = tuple(jnp.int32(value) for value in UNITS[0])
    lax.fori_loop(0, len(UNITS) // 2 - 1, body, first)
    score(UNITS[-1], s1, x1)
    mix(UNITS[-2], s0, x0)
    n_arrive(5)
    score_new(0, 0, s0, x0)
    mix(UNITS[-1], s1, x1)

    def late(i, carry):
        score_new(i, 1, s1, x1)
        mix_new(i, 0, s0, x0)

        @pl.when(i == LATE - 2)
        def _():
            n_arrive(6)
            n_arrive(7)

        score_new(jnp.minimum(i + 1, LATE - 1), 0, s0, x0)
        mix_new(i, 1, s1, x1)
        return carry

    lax.fori_loop(0, LATE, late, 0)

    for b in range(NQB):
        o_copy(b).wait_recv()
        own, lse = partials(0, b)
        other = ro[b, 0:DH, :].astype(F32)
        rows = ro[b, DH:OROWS, :].astype(F32)
        lse_other = rows[0:1] + rows[1:2] + rows[2:3]
        largest = jnp.maximum(lse, lse_other)
        e_own, e_other = jnp.exp2(lse - largest), jnp.exp2(lse_other - largest)
        share = 1.0 / (e_own + e_other)
        result = own * (e_own * share) + other * (e_other * share)
        for h in range(QB // DH):
            c = b * QB + h * DH
            out_ref[:, c:c + DH] = result[:, h * DH:(h + 1) * DH].T.astype(BF16)

    for d in range(2):
        for s in range(1, ZN):
            kv_copy(d, s).wait_send()
            n_copy(d, s).wait_send()
    w_copy.wait_send()
    for b in range(NQB):
        q_copy(b).wait_send()
        o_copy(b).wait_send()


def solution(mesh):
    freqs = 500000.0 ** (-(2.0 * np.arange(HALF, dtype=np.float64)) / DH)
    table = np.zeros((HALF, DH), np.float32)
    table[:, :HALF] = freqs[:, None]

    def part(q_new, k_new, v_new, k_cache, v_cache, new_pos):
        dma = pltpu.SemaphoreType.DMA
        return pl.pallas_call(
            kernel,
            out_shape=jax.ShapeDtypeStruct(q_new.shape, BF16),
            in_specs=[pl.BlockSpec(memory_space=pltpu.HBM)] * 7,
            out_specs=pl.BlockSpec(memory_space=pltpu.VMEM),
            scratch_shapes=[
                pltpu.VMEM((Q_ROWS, NQB * QB), BF16),
                pltpu.VMEM((NEW, DH), BF16),
                pltpu.VMEM((NEW, DH), BF16),
                pltpu.VMEM((OLD, DH), BF16),
                pltpu.VMEM((1, Q_ROWS), jnp.int32),
                pltpu.VMEM((HALF, DH), F32),
                dma((7 + NQB,)),
                pltpu.VMEM((2, NQB, DH, QB), BF16),
                pltpu.VMEM((ZN, 2 * SIZES[0], DH), BF16),
                pltpu.VMEM((ZN, 2 * SIZES[1], DH), BF16),
                pltpu.VMEM((2 * ZN, ROWS, DH), BF16),
                pltpu.VMEM((8, DH), F32),
                pltpu.VMEM((2, NCB, OROWS, CB), F32),
                pltpu.VMEM((2, NCB, 1, CB), F32),
                pltpu.VMEM((OLD, CB), F32),
                pltpu.VMEM((OLD, CB), F32),
                pltpu.VMEM((1, CB), F32),
                pltpu.VMEM((1, CB), F32),
                pltpu.VMEM((NQB, OROWS, QB), BF16),
                pltpu.VMEM((NQB, OROWS, QB), BF16),
                dma((2, ZN - 1)), dma((2, ZN - 1)),
                dma((2, ZN - 1)), dma((2, ZN - 1)),
                dma((NQB,)), dma((NQB,)), dma((NQB,)), dma((NQB,)),
                dma, dma,
            ],
            compiler_params=pltpu.CompilerParams(
                collective_id=0, has_side_effects=True, vmem_limit_bytes=64 << 20
            ),
        )(q_new, k_new, v_new, k_cache, v_cache, new_pos.reshape(1, -1), jnp.asarray(table))

    rows = P(("rep", "ctx"), "head")
    return jax.shard_map(
        part,
        mesh=mesh,
        in_specs=(rows,) * 5 + (P(("rep", "ctx")),),
        out_specs=rows,
        check_vma=False,
    )
```

```python
import math

import jax
import jax.numpy as jnp
import numpy as np
from jax import lax
from jax.experimental import pallas as pl
from jax.experimental.pallas import tpu as pltpu
from jax.sharding import PartitionSpec as P

DH = 128
HALF = 64
F32 = jnp.float32
BF16 = jnp.bfloat16
MESH = pl.DeviceIdType.MESH
LOG2E = math.log2(math.e)
SCALE = LOG2E / math.sqrt(DH)
NEG = -1e30
CACHED = 10240
Q_ROWS = 128

ZN = 8
SIZES = (384, 256)
OLD = 640
NEW = 128
QB = 512
NQB = 4
CB = 1024
NCB = 2
ROWS = 2 * NEW + 16
OROWS = DH + 16
OWN, OTHER = 0, 1
UNITS = (
    [(OWN, b, s) for s in (0, 1) for b in (0, 1)]
    + [(OTHER, 0, 0), (OTHER, 0, 1), (OWN, 0, 2), (OWN, 1, 2), (OTHER, 0, 2)]
    + [(OWN, 0, 3), (OWN, 1, 3), (OTHER, 0, 3)]
    + [(OTHER, 1, s) for s in range(4)]
    + [(OTHER, b, s) for s in (4, 5) for b in (0, 1)]
    + [(OWN, b, 4) for b in (0, 1)]
    + [(OTHER, b, s) for s in (6, 7) for b in (0, 1)]
    + [(OWN, b, s) for s in (5, 6, 7) for b in (0, 1)]
)
GROUP = 4
LATE = 2 * ZN // GROUP


def mm(a, b):
    return lax.dot_general(
        a, b, (((1,), (0,)), ((), ())), preferred_element_type=F32
    )


def turn(x, cosine, sine):
    lower, upper = x[:HALF], x[HALF:]
    return jnp.concatenate(
        [lower * cosine - upper * sine, upper * cosine + lower * sine], axis=0
    )


def kernel(
    q_hbm, kn_hbm, vn_hbm, kc_hbm, vc_hbm, pos_hbm, freq_hbm, out_hbm,
    out_ref, out_sem, q_ref, kn_ref, vn_ref, vc_ref, pos_ref, freq_ref, load_sem,
    qt, kva, kvb, nw, qp, acc, top, s0, s1, x0, x1, so, ro,
    k_send, k_recv, kv_send, kv_recv, n_send, n_recv, q_send, q_recv, o_send, o_recv, w_send, w_recv,
):
    ctx = lax.axis_index("ctx")
    head = lax.axis_index("head")
    hi, z = ctx // ZN, ctx % ZN
    right = {"ctx": hi * ZN + (z + 1) % ZN, "head": head}
    left = {"ctx": hi * ZN + (z + ZN - 1) % ZN, "head": head}
    partner = {"ctx": (1 - hi) * ZN + z, "head": head}
    everyone = (right, left, partner)

    barrier = pltpu.get_barrier_semaphore()
    for other in everyone:
        pl.semaphore_signal(barrier, inc=1, device_id=other, device_id_type=MESH)

    def load(src, dst, i):
        return pltpu.make_async_copy(src, dst, load_sem.at[i])

    vc_load = load(vc_hbm, vc_ref, 0)
    kc_loads = [
        load(kc_hbm.at[pl.ds(0, SIZES[0])], kva.at[0, pl.ds(0, SIZES[0])], 1),
        load(kc_hbm.at[pl.ds(SIZES[0], SIZES[1])], kvb.at[0, pl.ds(0, SIZES[1])], 2),
    ]
    pos_load = load(pos_hbm, pos_ref, 3)
    freq_load = load(freq_hbm, freq_ref, 4)
    kn_load = load(kn_hbm, kn_ref, 5)
    vn_load = load(vn_hbm, vn_ref, 6)
    q_loads = [
        load(q_hbm.at[:, pl.ds(b * QB, QB)], q_ref.at[:, pl.ds(b * QB, QB)], 7 + b)
        for b in range(NQB)
    ]
    for one in (vc_load, *kc_loads, pos_load, freq_load, *q_loads, kn_load, vn_load):
        one.start()

    def remote(src, dst, send, recv, target):
        return pltpu.make_async_remote_copy(
            src_ref=src, dst_ref=dst, send_sem=send, recv_sem=recv,
            device_id=target, device_id_type=MESH,
        )

    def held_in(d, s):
        return (kva, 0) if s % 2 == 1 - d else (kvb, 1)

    def own_keys(d, s):
        held, i = held_in(d, s)
        return remote(
            kc_hbm.at[pl.ds(i * SIZES[0], SIZES[i])], held.at[s, pl.ds(0, SIZES[i])],
            k_send.at[d, s - 1], k_recv.at[d, s - 1], right if d == 0 else left,
        )

    def kv_copy(d, s):
        held, i = held_in(d, s)
        if s <= 2:
            values = pl.ds(SIZES[i], SIZES[i])
            return remote(
                held.at[0, values], held.at[s, values], kv_send.at[d, s - 1],
                kv_recv.at[d, s - 1], right if d == 0 else left,
            )
        return remote(
            held.at[s - 2], held.at[s], kv_send.at[d, s - 1], kv_recv.at[d, s - 1],
            right if d == 0 else left,
        )

    def new_at(d, n):
        return 2 * n + d

    def n_copy(d, n):
        src = (n - 1 if d == 0 else 2 - n) if n <= 2 else new_at(d, n - 2)
        return remote(
            nw.at[src], nw.at[new_at(d, n)], n_send.at[d, n - 1], n_recv.at[d, n - 1],
            right if d == 0 else left,
        )

    def q_copy(b):
        return remote(qt.at[0, b], qt.at[1, b], q_send.at[b], q_recv.at[b], partner)

    def o_copy(b):
        return remote(so.at[b], ro.at[b], o_send.at[b], o_recv.at[b], partner)

    w_copy = remote(nw.at[0], nw.at[1], w_send, w_recv, partner)

    pl.semaphore_wait(barrier, len(everyone))
    for d in range(2):
        own_keys(d, 1).start()
    vc_load.wait()
    for t in range(3):
        kva[0, SIZES[0] + DH * t:SIZES[0] + DH * (t + 1), :] = (
            vc_ref[DH * t:DH * (t + 1), :].astype(F32).T.astype(BF16)
        )
    for t in range(2):
        r = SIZES[0] + DH * t
        kvb[0, SIZES[1] + DH * t:SIZES[1] + DH * (t + 1), :] = (
            vc_ref[r:r + DH, :].astype(F32).T.astype(BF16)
        )
    for d in range(2):
        kv_copy(d, 1).start()
    for d in range(2):
        own_keys(d, 2).start()
    for d in range(2):
        kv_copy(d, 2).start()
    for one in kc_loads:
        one.wait()

    pos_load.wait()
    freq_load.wait()
    positions = pos_ref[...].astype(F32)
    relative = positions - CACHED
    angle = freq_ref[:, 0:1] * positions
    cosine, sine = jnp.cos(angle), jnp.sin(angle)
    for b in range(NQB):
        q_loads[b].wait()
        for h in range(QB // DH):
            c = b * QB + h * DH
            x = q_ref[:, c:c + DH].astype(F32).T
            qt[0, b, :, h * DH:(h + 1) * DH] = turn(x, cosine, sine).astype(BF16)
        q_copy(b).start()
    acc[...] = jnp.zeros(acc.shape, F32)
    top[...] = jnp.full(top.shape, NEG, F32)
    qp[...] = jnp.broadcast_to(relative, (8, DH))
    kn_load.wait()
    vn_load.wait()
    nw[0, 0:NEW, :] = turn(kn_ref[...].astype(F32).T, cosine, sine).T.astype(BF16)
    nw[0, NEW:2 * NEW, :] = vn_ref[...].astype(F32).T.astype(BF16)
    number = [
        jnp.broadcast_to(relative[:, d * HALF:d * HALF + 1] * (1.0 / HALF), (8, DH))
        for d in range(2)
    ]
    nw[0, 2 * NEW:ROWS, :] = jnp.concatenate(number, axis=0).astype(BF16)

    def unit(u):
        found = []
        for field in zip(*UNITS):
            value = jnp.int32(field[0])
            for at in range(1, len(field)):
                if field[at] != field[at - 1]:
                    value = jnp.where(u >= at, field[at], value)
            found.append(value)
        return tuple(found)

    def queries(group, blk):
        return jnp.concatenate([qt[group, 2 * blk], qt[group, 2 * blk + 1]], axis=1)

    def score(at, s_ref, x_ref):
        group, blk, step = at
        q = queries(group, blk)
        k = jnp.concatenate(
            [kva[step, 0:SIZES[0], :], kvb[step, 0:SIZES[1], :]], axis=0
        )
        s = mm(k, q) * SCALE
        s_ref[0:OLD, :] = s
        x_ref[...] = jnp.max(s, axis=0, keepdims=True)

    def score_new(i, blk, s_ref, x_ref):
        q = queries(0, blk)
        qpos = qp[0:1]
        row = lax.broadcasted_iota(jnp.int32, (HALF, DH), 0).astype(F32)
        bias = []
        for j in range(GROUP):
            number = nw[i * GROUP + j, 2 * NEW:ROWS, :].astype(F32)
            for d in range(2):
                bias.append(jnp.where(number[8 * d:8 * d + 1] * HALF + row <= qpos, 0.0, NEG))
        bias = jnp.concatenate(bias, axis=0)
        k = jnp.concatenate([nw[i * GROUP + j, 0:NEW, :] for j in range(GROUP)], axis=0)
        s = mm(k, q) * SCALE + jnp.concatenate([bias] * (CB // DH), axis=1)
        s_ref[0:GROUP * NEW, :] = s
        x_ref[...] = jnp.max(s, axis=0, keepdims=True)

    def mix_in(group, blk, s, x_ref, tiles):
        before = top[group, blk]
        after = jnp.maximum(before, x_ref[...])
        top[group, blk] = after
        fade = jnp.exp2(before - after)
        p = jnp.exp2(s - after).astype(BF16)
        v = jnp.concatenate(tiles, axis=1)
        v = jnp.concatenate([v, jnp.ones((16, v.shape[1]), BF16)], axis=0)
        acc[group, blk] = acc[group, blk] * fade + mm(v, p)

    def mix(at, s_ref, x_ref):
        group, blk, step = at
        tiles = [
            held[step, size + DH * t:size + DH * (t + 1), :]
            for held, size in ((kva, SIZES[0]), (kvb, SIZES[1]))
            for t in range(size // DH)
        ]
        mix_in(group, blk, s_ref[0:OLD, :], x_ref, tiles)

    def mix_new(i, blk, s_ref, x_ref):
        tiles = [nw[i * GROUP + j, NEW:2 * NEW, :] for j in range(GROUP)]
        mix_in(0, blk, s_ref[0:GROUP * NEW, :], x_ref, tiles)

    def kv_arrive(s):
        for d in range(2):
            kv_copy(d, s).wait_recv()
            if s <= 2:
                own_keys(d, s).wait_recv()
            if s + 2 < ZN:
                kv_copy(d, s + 2).start()

    def n_arrive(n):
        for d in range(2):
            n_copy(d, n).wait_recv()
            if n + 2 < ZN:
                n_copy(d, n + 2).start()

    def partials(group, b):
        blk, c = b // 2, (b % 2) * QB
        a = acc[group, blk, :, c:c + QB]
        total = a[DH:DH + 1]
        lse = top[group, blk, :, c:c + QB] + jnp.log(total) * LOG2E
        return a[:DH] / total, lse

    def finish(b):
        o, lse = partials(1, b)
        so[b, 0:DH, :] = o.astype(BF16)
        high = lse.astype(BF16).astype(F32)
        middle = (lse - high).astype(BF16).astype(F32)
        low = lse - high - middle
        row = lax.broadcasted_iota(jnp.int32, (16, QB), 0)
        so[b, DH:OROWS, :] = jnp.where(
            row == 0, high, jnp.where(row == 1, middle, low)
        ).astype(BF16)
        o_copy(b).start()

    def q_arrive(b):
        q_copy(b).wait_recv()

    def w_begin():
        w_copy.start()

    def n_begin():
        w_copy.wait_recv()
        for n in (1, 2):
            for d in range(2):
                n_copy(d, n).start()

    after = {
        0: [(kv_arrive, 1)],
        2: [(q_arrive, 0), (q_arrive, 1)],
        4: [(kv_arrive, 2)],
        7: [(kv_arrive, 3)],
        10: [(q_arrive, 2), (q_arrive, 3), (w_begin,)],
        11: [(kv_arrive, 4)],
        15: [(kv_arrive, 5), (n_begin,)],
        19: [(kv_arrive, 6)],
        22: [(kv_arrive, 7)],
        24: [(finish, 0), (finish, 1), (n_arrive, 1)],
        25: [(finish, 2), (finish, 3)],
        26: [(n_arrive, 2)],
        28: [(n_arrive, 3)],
    }

    def sync(u, odd):
        for at, actions in after.items():
            if at % 2 == odd:
                @pl.when(u == at)
                def _(actions=actions):
                    for action, *given in actions:
                        action(*given)

    score(UNITS[0], s0, x0)

    def body(i, now):
        u = 2 * i
        then = unit(u + 1)
        score(then, s1, x1)
        mix(now, s0, x0)
        sync(u, 0)
        now = unit(u + 2)
        score(now, s0, x0)
        mix(then, s1, x1)
        sync(u + 1, 1)
        return now

    first = tuple(jnp.int32(value) for value in UNITS[0])
    lax.fori_loop(0, len(UNITS) // 2 - 1, body, first)
    score(UNITS[-1], s1, x1)
    mix(UNITS[-2], s0, x0)
    n_arrive(4)
    score_new(0, 0, s0, x0)
    mix(UNITS[-1], s1, x1)

    def late(i, carry):
        score_new(i, 1, s1, x1)
        mix_new(i, 0, s0, x0)

        @pl.when(i == 0)
        def _():
            n_arrive(5)

        @pl.when(i == LATE - 2)
        def _():
            n_arrive(6)
            n_arrive(7)

        score_new(i + 1, 0, s0, x0)
        mix_new(i, 1, s1, x1)
        return carry

    def out_copy(b):
        return pltpu.make_async_copy(
            out_ref.at[:, pl.ds(b * QB, QB)], out_hbm.at[:, pl.ds(b * QB, QB)], out_sem.at[b]
        )

    def result(b):
        own, lse = partials(0, b)
        other = ro[b, 0:DH, :].astype(F32)
        rows = ro[b, DH:OROWS, :].astype(F32)
        lse_other = rows[0:1] + rows[1:2] + rows[2:3]
        largest = jnp.maximum(lse, lse_other)
        e_own, e_other = jnp.exp2(lse - largest), jnp.exp2(lse_other - largest)
        share = 1.0 / (e_own + e_other)
        mixed = own * (e_own * share) + other * (e_other * share)
        for h in range(QB // DH):
            c = b * QB + h * DH
            out_ref[:, c:c + DH] = mixed[:, h * DH:(h + 1) * DH].T.astype(BF16)
        out_copy(b).start()

    lax.fori_loop(0, LATE - 1, late, 0)
    score_new(LATE - 1, 1, s1, x1)
    mix_new(LATE - 1, 0, s0, x0)
    for b in (0, 1):
        o_copy(b).wait_recv()
    mix_new(LATE - 1, 1, s1, x1)
    result(0)
    result(1)
    for b in (2, 3):
        o_copy(b).wait_recv()
        result(b)

    for d in range(2):
        for s in range(1, ZN):
            kv_copy(d, s).wait_send()
            if s <= 2:
                own_keys(d, s).wait_send()
            n_copy(d, s).wait_send()
    w_copy.wait_send()
    for b in range(NQB):
        out_copy(b).wait()
    for b in range(NQB):
        q_copy(b).wait_send()
        o_copy(b).wait_send()


def solution(mesh):
    freqs = 500000.0 ** (-(2.0 * np.arange(HALF, dtype=np.float64)) / DH)
    table = np.zeros((HALF, DH), np.float32)
    table[:, :HALF] = freqs[:, None]

    def part(q_new, k_new, v_new, k_cache, v_cache, new_pos):
        dma = pltpu.SemaphoreType.DMA
        return pl.pallas_call(
            kernel,
            out_shape=jax.ShapeDtypeStruct(q_new.shape, BF16),
            in_specs=[pl.BlockSpec(memory_space=pltpu.HBM)] * 7,
            out_specs=pl.BlockSpec(memory_space=pltpu.HBM),
            scratch_shapes=[
                pltpu.VMEM((Q_ROWS, NQB * QB), BF16),
                dma((NQB,)),
                pltpu.VMEM((Q_ROWS, NQB * QB), BF16),
                pltpu.VMEM((NEW, DH), BF16),
                pltpu.VMEM((NEW, DH), BF16),
                pltpu.VMEM((OLD, DH), BF16),
                pltpu.VMEM((1, Q_ROWS), jnp.int32),
                pltpu.VMEM((HALF, DH), F32),
                dma((7 + NQB,)),
                pltpu.VMEM((2, NQB, DH, QB), BF16),
                pltpu.VMEM((ZN, 2 * SIZES[0], DH), BF16),
                pltpu.VMEM((ZN, 2 * SIZES[1], DH), BF16),
                pltpu.VMEM((2 * ZN, ROWS, DH), BF16),
                pltpu.VMEM((8, DH), F32),
                pltpu.VMEM((2, NCB, OROWS, CB), F32),
                pltpu.VMEM((2, NCB, 1, CB), F32),
                pltpu.VMEM((OLD, CB), F32),
                pltpu.VMEM((OLD, CB), F32),
                pltpu.VMEM((1, CB), F32),
                pltpu.VMEM((1, CB), F32),
                pltpu.VMEM((NQB, OROWS, QB), BF16),
                pltpu.VMEM((NQB, OROWS, QB), BF16),
                dma((2, 2)), dma((2, 2)),
                dma((2, ZN - 1)), dma((2, ZN - 1)),
                dma((2, ZN - 1)), dma((2, ZN - 1)),
                dma((NQB,)), dma((NQB,)), dma((NQB,)), dma((NQB,)),
                dma, dma,
            ],
            compiler_params=pltpu.CompilerParams(
                collective_id=0, has_side_effects=True, vmem_limit_bytes=64 << 20
            ),
        )(q_new, k_new, v_new, k_cache, v_cache, new_pos.reshape(1, -1), jnp.asarray(table))

    rows = P(("rep", "ctx"), "head")
    return jax.shard_map(
        part,
        mesh=mesh,
        in_specs=(rows,) * 5 + (P(("rep", "ctx")),),
        out_specs=rows,
        check_vma=False,
    )
```

```python
import math

import jax
import jax.numpy as jnp
import numpy as np
from jax import lax
from jax.experimental import pallas as pl
from jax.experimental.pallas import tpu as pltpu
from jax.sharding import PartitionSpec as P

DH = 128
HALF = 64
F32 = jnp.float32
BF16 = jnp.bfloat16
MESH = pl.DeviceIdType.MESH
LOG2E = math.log2(math.e)
SCALE = LOG2E / math.sqrt(DH)
NEG = -1e30
CACHED = 10240
Q_ROWS = 128

ZN = 8
SIZES = (384, 256)
OLD = 640
NEW = 128
QB = 512
NQB = 4
CB = 1024
NCB = 2
ROWS = 2 * NEW + 16
OROWS = DH + 16
OWN, OTHER = 0, 1
UNITS = (
    [(OWN, b, s) for s in (0, 1) for b in (0, 1)]
    + [(OTHER, 0, 0), (OTHER, 0, 1), (OWN, 0, 2), (OWN, 1, 2), (OTHER, 0, 2)]
    + [(OWN, 0, 3), (OWN, 1, 3), (OTHER, 0, 3)]
    + [(OTHER, 1, s) for s in range(4)]
    + [(OTHER, b, s) for s in (4, 5) for b in (0, 1)]
    + [(OWN, b, 4) for b in (0, 1)]
    + [(OTHER, b, s) for s in (6, 7) for b in (0, 1)]
    + [(OWN, b, s) for s in (5, 6, 7) for b in (0, 1)]
)
GROUP = 4
LATE = 2 * ZN // GROUP


def mm(a, b):
    return lax.dot_general(
        a, b, (((1,), (0,)), ((), ())), preferred_element_type=F32
    )


def turn(x, cosine, sine):
    lower, upper = x[:HALF], x[HALF:]
    return jnp.concatenate(
        [lower * cosine - upper * sine, upper * cosine + lower * sine], axis=0
    )


def kernel(
    q_hbm, kn_hbm, vn_hbm, kc_hbm, vc_hbm, pos_hbm, freq_hbm, out_hbm,
    out_ref, out_sem, q_ref, kn_ref, vn_ref, vc_ref, pos_ref, freq_ref, load_sem,
    qt, kva, kvb, nw, qp, acc, top, s0, s1, x0, x1, so, ro,
    k_send, k_recv, kv_send, kv_recv, n_send, n_recv, q_send, q_recv, o_send, o_recv, w_send, w_recv,
):
    ctx = lax.axis_index("ctx")
    head = lax.axis_index("head")
    hi, z = ctx // ZN, ctx % ZN
    right = {"ctx": hi * ZN + (z + 1) % ZN, "head": head}
    left = {"ctx": hi * ZN + (z + ZN - 1) % ZN, "head": head}
    partner = {"ctx": (1 - hi) * ZN + z, "head": head}
    everyone = (right, left, partner)

    barrier = pltpu.get_barrier_semaphore()
    for other in everyone:
        pl.semaphore_signal(barrier, inc=1, device_id=other, device_id_type=MESH)

    def load(src, dst, i):
        return pltpu.make_async_copy(src, dst, load_sem.at[i])

    vc_load = load(vc_hbm, vc_ref, 0)
    kc_loads = [
        load(kc_hbm.at[pl.ds(0, SIZES[0])], kva.at[0, pl.ds(0, SIZES[0])], 1),
        load(kc_hbm.at[pl.ds(SIZES[0], SIZES[1])], kvb.at[0, pl.ds(0, SIZES[1])], 2),
    ]
    pos_load = load(pos_hbm, pos_ref, 3)
    freq_load = load(freq_hbm, freq_ref, 4)
    kn_load = load(kn_hbm, kn_ref, 5)
    vn_load = load(vn_hbm, vn_ref, 6)
    q_loads = [
        load(q_hbm.at[:, pl.ds(b * QB, QB)], q_ref.at[:, pl.ds(b * QB, QB)], 7 + b)
        for b in range(NQB)
    ]
    for one in (vc_load, *kc_loads, pos_load, freq_load, *q_loads, kn_load, vn_load):
        one.start()

    def remote(src, dst, send, recv, target):
        return pltpu.make_async_remote_copy(
            src_ref=src, dst_ref=dst, send_sem=send, recv_sem=recv,
            device_id=target, device_id_type=MESH,
        )

    def held_in(d, s):
        return (kva, 0) if s % 2 == 1 - d else (kvb, 1)

    def own_keys(d, s):
        held, i = held_in(d, s)
        return remote(
            kc_hbm.at[pl.ds(i * SIZES[0], SIZES[i])], held.at[s, pl.ds(0, SIZES[i])],
            k_send.at[d, s - 1], k_recv.at[d, s - 1], right if d == 0 else left,
        )

    def kv_copy(d, s):
        held, i = held_in(d, s)
        if s <= 2:
            values = pl.ds(SIZES[i], SIZES[i])
            return remote(
                held.at[0, values], held.at[s, values], kv_send.at[d, s - 1],
                kv_recv.at[d, s - 1], right if d == 0 else left,
            )
        return remote(
            held.at[s - 2], held.at[s], kv_send.at[d, s - 1], kv_recv.at[d, s - 1],
            right if d == 0 else left,
        )

    def new_at(d, n):
        return 2 * n + d

    def n_copy(d, n):
        src = (n - 1 if d == 0 else 2 - n) if n <= 2 else new_at(d, n - 2)
        return remote(
            nw.at[src], nw.at[new_at(d, n)], n_send.at[d, n - 1], n_recv.at[d, n - 1],
            right if d == 0 else left,
        )

    def q_copy(b):
        return remote(qt.at[0, b], qt.at[1, b], q_send.at[b], q_recv.at[b], partner)

    def o_copy(b):
        return remote(so.at[b], ro.at[b], o_send.at[b], o_recv.at[b], partner)

    w_copy = remote(nw.at[0], nw.at[1], w_send, w_recv, partner)

    pl.semaphore_wait(barrier, len(everyone))
    for d in range(2):
        own_keys(d, 1).start()
    vc_load.wait()
    for t in range(3):
        kva[0, SIZES[0] + DH * t:SIZES[0] + DH * (t + 1), :] = (
            vc_ref[DH * t:DH * (t + 1), :].astype(F32).T.astype(BF16)
        )
    for t in range(2):
        r = SIZES[0] + DH * t
        kvb[0, SIZES[1] + DH * t:SIZES[1] + DH * (t + 1), :] = (
            vc_ref[r:r + DH, :].astype(F32).T.astype(BF16)
        )
    for d in range(2):
        kv_copy(d, 1).start()
    for d in range(2):
        own_keys(d, 2).start()
    for d in range(2):
        kv_copy(d, 2).start()
    for one in kc_loads:
        one.wait()

    pos_load.wait()
    freq_load.wait()
    positions = pos_ref[...].astype(F32)
    relative = positions - CACHED
    angle = freq_ref[:, 0:1] * positions
    cosine, sine = jnp.cos(angle), jnp.sin(angle)
    for b in range(NQB):
        q_loads[b].wait()
        for h in range(QB // DH):
            c = b * QB + h * DH
            x = q_ref[:, c:c + DH].astype(F32).T
            qt[0, b, :, h * DH:(h + 1) * DH] = turn(x, cosine, sine).astype(BF16)
        q_copy(b).start()
    acc[...] = jnp.zeros(acc.shape, F32)
    top[...] = jnp.full(top.shape, NEG, F32)
    qp[...] = jnp.broadcast_to(relative, (8, DH))
    kn_load.wait()
    vn_load.wait()
    nw[0, 0:NEW, :] = turn(kn_ref[...].astype(F32).T, cosine, sine).T.astype(BF16)
    nw[0, NEW:2 * NEW, :] = vn_ref[...].astype(F32).T.astype(BF16)
    number = [
        jnp.broadcast_to(relative[:, d * HALF:d * HALF + 1] * (1.0 / HALF), (8, DH))
        for d in range(2)
    ]
    nw[0, 2 * NEW:ROWS, :] = jnp.concatenate(number, axis=0).astype(BF16)

    def unit(u):
        found = []
        for field in zip(*UNITS):
            value = jnp.int32(field[0])
            for at in range(1, len(field)):
                if field[at] != field[at - 1]:
                    value = jnp.where(u >= at, field[at], value)
            found.append(value)
        return tuple(found)

    def queries(group, blk):
        return jnp.concatenate([qt[group, 2 * blk], qt[group, 2 * blk + 1]], axis=1)

    def score(at, s_ref, x_ref):
        group, blk, step = at
        q = queries(group, blk)
        k = jnp.concatenate(
            [kva[step, 0:SIZES[0], :], kvb[step, 0:SIZES[1], :]], axis=0
        )
        s = mm(k, q) * SCALE
        s_ref[0:OLD, :] = s
        x_ref[...] = jnp.max(s, axis=0, keepdims=True)

    def score_new(i, blk, s_ref, x_ref, first=0, count=GROUP):
        q = queries(0, blk)
        qpos = qp[0:1]
        row = lax.broadcasted_iota(jnp.int32, (HALF, DH), 0).astype(F32)
        bias = []
        for j in range(first, first + count):
            number = nw[i * GROUP + j, 2 * NEW:ROWS, :].astype(F32)
            for d in range(2):
                bias.append(jnp.where(number[8 * d:8 * d + 1] * HALF + row <= qpos, 0.0, NEG))
        bias = jnp.concatenate(bias, axis=0)
        k = jnp.concatenate([nw[i * GROUP + j, 0:NEW, :] for j in range(first, first + count)], axis=0)
        s = mm(k, q) * SCALE + jnp.concatenate([bias] * (CB // DH), axis=1)
        s_ref[0:count * NEW, :] = s
        x_ref[...] = jnp.max(s, axis=0, keepdims=True)

    def mix_in(group, blk, s, x_ref, tiles):
        before = top[group, blk]
        after = jnp.maximum(before, x_ref[...])
        top[group, blk] = after
        fade = jnp.exp2(before - after)
        p = jnp.exp2(s - after).astype(BF16)
        v = jnp.concatenate(tiles, axis=1)
        v = jnp.concatenate([v, jnp.ones((16, v.shape[1]), BF16)], axis=0)
        acc[group, blk] = acc[group, blk] * fade + mm(v, p)

    def mix(at, s_ref, x_ref):
        group, blk, step = at
        tiles = [
            held[step, size + DH * t:size + DH * (t + 1), :]
            for held, size in ((kva, SIZES[0]), (kvb, SIZES[1]))
            for t in range(size // DH)
        ]
        mix_in(group, blk, s_ref[0:OLD, :], x_ref, tiles)

    def mix_new(i, blk, s_ref, x_ref, first=0, count=GROUP):
        tiles = [nw[i * GROUP + j, NEW:2 * NEW, :] for j in range(first, first + count)]
        mix_in(0, blk, s_ref[0:count * NEW, :], x_ref, tiles)

    def kv_arrive(s):
        for d in range(2):
            kv_copy(d, s).wait_recv()
            if s <= 2:
                own_keys(d, s).wait_recv()
            if s + 2 < ZN:
                kv_copy(d, s + 2).start()

    def n_arrive(n):
        for d in range(2):
            n_copy(d, n).wait_recv()
            if n + 2 < ZN:
                n_copy(d, n + 2).start()

    def partials(group, b):
        blk, c = b // 2, (b % 2) * QB
        a = acc[group, blk, :, c:c + QB]
        total = a[DH:DH + 1]
        lse = top[group, blk, :, c:c + QB] + jnp.log(total) * LOG2E
        return a[:DH] / total, lse

    def finish(b):
        o, lse = partials(1, b)
        so[b, 0:DH, :] = o.astype(BF16)
        high = lse.astype(BF16).astype(F32)
        middle = (lse - high).astype(BF16).astype(F32)
        low = lse - high - middle
        row = lax.broadcasted_iota(jnp.int32, (16, QB), 0)
        so[b, DH:OROWS, :] = jnp.where(
            row == 0, high, jnp.where(row == 1, middle, low)
        ).astype(BF16)
        o_copy(b).start()

    def q_arrive(b):
        q_copy(b).wait_recv()

    def w_begin():
        w_copy.start()

    def n_begin():
        w_copy.wait_recv()
        for n in (1, 2):
            for d in range(2):
                n_copy(d, n).start()

    after = {
        0: [(kv_arrive, 1)],
        2: [(q_arrive, 0), (q_arrive, 1)],
        4: [(kv_arrive, 2)],
        7: [(kv_arrive, 3)],
        10: [(q_arrive, 2), (q_arrive, 3), (w_begin,)],
        11: [(kv_arrive, 4)],
        15: [(kv_arrive, 5), (n_begin,)],
        19: [(kv_arrive, 6)],
        22: [(kv_arrive, 7)],
        24: [(finish, 0), (finish, 1), (n_arrive, 1)],
        25: [(finish, 2), (finish, 3)],
        26: [(n_arrive, 2)],
        28: [(n_arrive, 3)],
    }

    def sync(u, odd):
        for at, actions in after.items():
            if at % 2 == odd:
                @pl.when(u == at)
                def _(actions=actions):
                    for action, *given in actions:
                        action(*given)

    score(UNITS[0], s0, x0)

    def body(i, now):
        u = 2 * i
        then = unit(u + 1)
        score(then, s1, x1)
        mix(now, s0, x0)
        sync(u, 0)
        now = unit(u + 2)
        score(now, s0, x0)
        mix(then, s1, x1)
        sync(u + 1, 1)
        return now

    first = tuple(jnp.int32(value) for value in UNITS[0])
    lax.fori_loop(0, len(UNITS) // 2 - 1, body, first)
    score(UNITS[-1], s1, x1)
    mix(UNITS[-2], s0, x0)
    n_arrive(4)
    score_new(0, 0, s0, x0)
    mix(UNITS[-1], s1, x1)

    def late(i, carry):
        score_new(i, 1, s1, x1)
        mix_new(i, 0, s0, x0)

        @pl.when(i == 0)
        def _():
            n_arrive(5)

        score_new(i + 1, 0, s0, x0)
        mix_new(i, 1, s1, x1)
        return carry

    def out_copy(b):
        return pltpu.make_async_copy(
            out_ref.at[:, pl.ds(b * QB, QB)], out_hbm.at[:, pl.ds(b * QB, QB)], out_sem.at[b]
        )

    def result(b):
        own, lse = partials(0, b)
        other = ro[b, 0:DH, :].astype(F32)
        rows = ro[b, DH:OROWS, :].astype(F32)
        lse_other = rows[0:1] + rows[1:2] + rows[2:3]
        largest = jnp.maximum(lse, lse_other)
        e_own, e_other = jnp.exp2(lse - largest), jnp.exp2(lse_other - largest)
        share = 1.0 / (e_own + e_other)
        mixed = own * (e_own * share) + other * (e_other * share)
        for h in range(QB // DH):
            c = b * QB + h * DH
            out_ref[:, c:c + DH] = mixed[:, h * DH:(h + 1) * DH].T.astype(BF16)
        out_copy(b).start()

    lax.fori_loop(0, LATE - 2, late, 0)
    end, half = LATE - 1, GROUP // 2
    score_new(end - 1, 1, s1, x1)
    mix_new(end - 1, 0, s0, x0)
    n_arrive(6)
    score_new(end, 0, s0, x0, 0, half)
    mix_new(end - 1, 1, s1, x1)
    score_new(end, 1, s1, x1, 0, half)
    mix_new(end, 0, s0, x0, 0, half)
    n_arrive(7)
    score_new(end, 0, s0, x0, half, half)
    mix_new(end, 1, s1, x1, 0, half)
    score_new(end, 1, s1, x1, half, half)
    mix_new(end, 0, s0, x0, half, half)
    for b in (0, 1):
        o_copy(b).wait_recv()
    mix_new(end, 1, s1, x1, half, half)
    result(0)
    result(1)
    for b in (2, 3):
        o_copy(b).wait_recv()
        result(b)

    for d in range(2):
        for s in range(1, ZN):
            kv_copy(d, s).wait_send()
            if s <= 2:
                own_keys(d, s).wait_send()
            n_copy(d, s).wait_send()
    w_copy.wait_send()
    for b in range(NQB):
        out_copy(b).wait()
    for b in range(NQB):
        q_copy(b).wait_send()
        o_copy(b).wait_send()


def solution(mesh):
    freqs = 500000.0 ** (-(2.0 * np.arange(HALF, dtype=np.float64)) / DH)
    table = np.zeros((HALF, DH), np.float32)
    table[:, :HALF] = freqs[:, None]

    def part(q_new, k_new, v_new, k_cache, v_cache, new_pos):
        dma = pltpu.SemaphoreType.DMA
        return pl.pallas_call(
            kernel,
            out_shape=jax.ShapeDtypeStruct(q_new.shape, BF16),
            in_specs=[pl.BlockSpec(memory_space=pltpu.HBM)] * 7,
            out_specs=pl.BlockSpec(memory_space=pltpu.HBM),
            scratch_shapes=[
                pltpu.VMEM((Q_ROWS, NQB * QB), BF16),
                dma((NQB,)),
                pltpu.VMEM((Q_ROWS, NQB * QB), BF16),
                pltpu.VMEM((NEW, DH), BF16),
                pltpu.VMEM((NEW, DH), BF16),
                pltpu.VMEM((OLD, DH), BF16),
                pltpu.VMEM((1, Q_ROWS), jnp.int32),
                pltpu.VMEM((HALF, DH), F32),
                dma((7 + NQB,)),
                pltpu.VMEM((2, NQB, DH, QB), BF16),
                pltpu.VMEM((ZN, 2 * SIZES[0], DH), BF16),
                pltpu.VMEM((ZN, 2 * SIZES[1], DH), BF16),
                pltpu.VMEM((2 * ZN, ROWS, DH), BF16),
                pltpu.VMEM((8, DH), F32),
                pltpu.VMEM((2, NCB, OROWS, CB), F32),
                pltpu.VMEM((2, NCB, 1, CB), F32),
                pltpu.VMEM((OLD, CB), F32),
                pltpu.VMEM((OLD, CB), F32),
                pltpu.VMEM((1, CB), F32),
                pltpu.VMEM((1, CB), F32),
                pltpu.VMEM((NQB, OROWS, QB), BF16),
                pltpu.VMEM((NQB, OROWS, QB), BF16),
                dma((2, 2)), dma((2, 2)),
                dma((2, ZN - 1)), dma((2, ZN - 1)),
                dma((2, ZN - 1)), dma((2, ZN - 1)),
                dma((NQB,)), dma((NQB,)), dma((NQB,)), dma((NQB,)),
                dma, dma,
            ],
            compiler_params=pltpu.CompilerParams(
                collective_id=0, has_side_effects=True, vmem_limit_bytes=64 << 20
            ),
        )(q_new, k_new, v_new, k_cache, v_cache, new_pos.reshape(1, -1), jnp.asarray(table))

    rows = P(("rep", "ctx"), "head")
    return jax.shard_map(
        part,
        mesh=mesh,
        in_specs=(rows,) * 5 + (P(("rep", "ctx")),),
        out_specs=rows,
        check_vma=False,
    )
```

```python
import functools
import math

import jax
import jax.numpy as jnp
import numpy as np
from jax import lax
from jax.experimental import pallas as pl
from jax.experimental.pallas import tpu as pltpu
from jax.sharding import PartitionSpec as P

DH = 128
HALF = 64
F32 = jnp.float32
BF16 = jnp.bfloat16
MESH = pl.DeviceIdType.MESH
LOG2E = math.log2(math.e)
SCALE = LOG2E / math.sqrt(DH)
NEG = -1e30
CACHED = 10240
Q_ROWS = 128

ZN = 8
SIZES = (384, 256)
OLD = 640
NEW = 128
QB = 512
NQB = 4
CB = 1024
NCB = 2
ROWS = 2 * NEW + 16
OROWS = DH + 16
OWN, OTHER = 0, 1
UNITS = (
    [(OWN, b, s) for s in (0, 1) for b in (0, 1)]
    + [(OTHER, 0, 0), (OTHER, 0, 1), (OWN, 0, 2), (OWN, 1, 2), (OTHER, 0, 2)]
    + [(OWN, 0, 3), (OWN, 1, 3), (OTHER, 0, 3)]
    + [(OTHER, 1, s) for s in range(4)]
    + [(OTHER, b, s) for s in (4, 5) for b in (0, 1)]
    + [(OWN, b, 4) for b in (0, 1)]
    + [(OTHER, b, s) for s in (6, 7) for b in (0, 1)]
    + [(OWN, b, s) for s in (5, 6, 7) for b in (0, 1)]
)
GROUP = 4
LATE = 2 * ZN // GROUP


def mm(a, b):
    return lax.dot_general(
        a, b, (((1,), (0,)), ((), ())), preferred_element_type=F32
    )


def turn(x, cosine, sine):
    lower, upper = x[:HALF], x[HALF:]
    return jnp.concatenate(
        [lower * cosine - upper * sine, upper * cosine + lower * sine], axis=0
    )


def kernel(
    q_hbm, kn_hbm, vn_hbm, kc_hbm, vc_hbm, pos_hbm, freq_hbm, out_hbm,
    out_ref, out_sem, q_ref, kn_ref, vn_ref, vc_ref, pos_ref, freq_ref, load_sem,
    qt, kva, kvb, nw, qp, acc, top, s0, s1, x0, x1, so, ro,
    k_send, k_recv, kv_send, kv_recv, n_send, n_recv, q_send, q_recv, o_send, o_recv, w_send, w_recv,
):
    ctx = lax.axis_index("ctx")
    head = lax.axis_index("head")
    hi, z = ctx // ZN, ctx % ZN
    right = {"ctx": hi * ZN + (z + 1) % ZN, "head": head}
    left = {"ctx": hi * ZN + (z + ZN - 1) % ZN, "head": head}
    partner = {"ctx": (1 - hi) * ZN + z, "head": head}
    everyone = (right, left, partner)

    barrier = pltpu.get_barrier_semaphore()
    for other in everyone:
        pl.semaphore_signal(barrier, inc=1, device_id=other, device_id_type=MESH)

    def load(src, dst, i):
        return pltpu.make_async_copy(src, dst, load_sem.at[i])

    vc_load = load(vc_hbm, vc_ref, 0)
    kc_loads = [
        load(kc_hbm.at[pl.ds(0, SIZES[0])], kva.at[0, pl.ds(0, SIZES[0])], 1),
        load(kc_hbm.at[pl.ds(SIZES[0], SIZES[1])], kvb.at[0, pl.ds(0, SIZES[1])], 2),
    ]
    pos_load = load(pos_hbm, pos_ref, 3)
    freq_load = load(freq_hbm, freq_ref, 4)
    kn_load = load(kn_hbm, kn_ref, 5)
    vn_load = load(vn_hbm, vn_ref, 6)
    q_loads = [
        load(q_hbm.at[:, pl.ds(b * QB, QB)], q_ref.at[:, pl.ds(b * QB, QB)], 7 + b)
        for b in range(NQB)
    ]
    for one in (vc_load, *kc_loads, pos_load, freq_load, *q_loads, kn_load, vn_load):
        one.start()

    def remote(src, dst, send, recv, target):
        return pltpu.make_async_remote_copy(
            src_ref=src, dst_ref=dst, send_sem=send, recv_sem=recv,
            device_id=target, device_id_type=MESH,
        )

    def held_in(d, s):
        return (kva, 0) if s % 2 == 1 - d else (kvb, 1)

    def own_keys(d, s):
        held, i = held_in(d, s)
        return remote(
            kc_hbm.at[pl.ds(i * SIZES[0], SIZES[i])], held.at[s, pl.ds(0, SIZES[i])],
            k_send.at[d, s - 1], k_recv.at[d, s - 1], right if d == 0 else left,
        )

    def kv_copy(d, s):
        held, i = held_in(d, s)
        if s <= 2:
            values = pl.ds(SIZES[i], SIZES[i])
            return remote(
                held.at[0, values], held.at[s, values], kv_send.at[d, s - 1],
                kv_recv.at[d, s - 1], right if d == 0 else left,
            )
        return remote(
            held.at[s - 2], held.at[s], kv_send.at[d, s - 1], kv_recv.at[d, s - 1],
            right if d == 0 else left,
        )

    def new_at(d, n):
        return 2 * n + d

    def n_copy(d, n):
        src = (n - 1 if d == 0 else 2 - n) if n <= 2 else new_at(d, n - 2)
        return remote(
            nw.at[src], nw.at[new_at(d, n)], n_send.at[d, n - 1], n_recv.at[d, n - 1],
            right if d == 0 else left,
        )

    def q_copy(b):
        return remote(qt.at[0, b], qt.at[1, b], q_send.at[b], q_recv.at[b], partner)

    def o_copy(b):
        return remote(so.at[b], ro.at[b], o_send.at[b], o_recv.at[b], partner)

    w_copy = remote(nw.at[0], nw.at[1], w_send, w_recv, partner)

    pl.semaphore_wait(barrier, len(everyone))
    for d in range(2):
        own_keys(d, 1).start()
    vc_load.wait()
    for t in range(3):
        kva[0, SIZES[0] + DH * t:SIZES[0] + DH * (t + 1), :] = (
            vc_ref[DH * t:DH * (t + 1), :].astype(F32).T.astype(BF16)
        )
    for t in range(2):
        r = SIZES[0] + DH * t
        kvb[0, SIZES[1] + DH * t:SIZES[1] + DH * (t + 1), :] = (
            vc_ref[r:r + DH, :].astype(F32).T.astype(BF16)
        )
    for d in range(2):
        kv_copy(d, 1).start()
    for d in range(2):
        own_keys(d, 2).start()
    for d in range(2):
        kv_copy(d, 2).start()
    for one in kc_loads:
        one.wait()

    pos_load.wait()
    freq_load.wait()
    positions = pos_ref[...].astype(F32)
    relative = positions - CACHED
    angle = freq_ref[:, 0:1] * positions
    cosine, sine = jnp.cos(angle), jnp.sin(angle)
    for b in range(NQB):
        q_loads[b].wait()
        for h in range(QB // DH):
            c = b * QB + h * DH
            x = q_ref[:, c:c + DH].astype(F32).T
            qt[0, b, :, h * DH:(h + 1) * DH] = turn(x, cosine, sine).astype(BF16)
        q_copy(b).start()
    acc[...] = jnp.zeros(acc.shape, F32)
    top[...] = jnp.full(top.shape, NEG, F32)
    qp[...] = jnp.broadcast_to(relative, (8, DH))
    kn_load.wait()
    vn_load.wait()
    nw[0, 0:NEW, :] = turn(kn_ref[...].astype(F32).T, cosine, sine).T.astype(BF16)
    nw[0, NEW:2 * NEW, :] = vn_ref[...].astype(F32).T.astype(BF16)
    number = [
        jnp.broadcast_to(relative[:, d * HALF:d * HALF + 1] * (1.0 / HALF), (8, DH))
        for d in range(2)
    ]
    nw[0, 2 * NEW:ROWS, :] = jnp.concatenate(number, axis=0).astype(BF16)

    def unit(u):
        found = []
        for field in zip(*UNITS):
            value = jnp.int32(field[0])
            for at in range(1, len(field)):
                if field[at] != field[at - 1]:
                    value = jnp.where(u >= at, field[at], value)
            found.append(value)
        return tuple(found)

    def queries(group, blk):
        return jnp.concatenate([qt[group, 2 * blk], qt[group, 2 * blk + 1]], axis=1)

    def score(at, s_ref, x_ref):
        group, blk, step = at
        q = queries(group, blk)
        k = jnp.concatenate(
            [kva[step, 0:SIZES[0], :], kvb[step, 0:SIZES[1], :]], axis=0
        )
        s = mm(k, q) * SCALE
        s_ref[0:OLD, :] = s
        x_ref[...] = jnp.max(s, axis=0, keepdims=True)

    def score_new(i, blk, s_ref, x_ref, first=0, count=GROUP):
        q = queries(0, blk)
        qpos = qp[0:1]
        row = lax.broadcasted_iota(jnp.int32, (HALF, DH), 0).astype(F32)
        bias = []
        for j in range(first, first + count):
            number = nw[i * GROUP + j, 2 * NEW:ROWS, :].astype(F32)
            for d in range(2):
                bias.append(jnp.where(number[8 * d:8 * d + 1] * HALF + row <= qpos, 0.0, NEG))
        bias = jnp.concatenate(bias, axis=0)
        k = jnp.concatenate([nw[i * GROUP + j, 0:NEW, :] for j in range(first, first + count)], axis=0)
        s = mm(k, q) * SCALE + jnp.concatenate([bias] * (CB // DH), axis=1)
        s_ref[0:count * NEW, :] = s
        x_ref[...] = jnp.max(s, axis=0, keepdims=True)

    def mix_in(group, blk, s, x_ref, tiles):
        before = top[group, blk]
        after = jnp.maximum(before, x_ref[...])
        top[group, blk] = after
        fade = jnp.exp2(before - after)
        p = jnp.exp2(s - after).astype(BF16)
        v = jnp.concatenate(tiles, axis=1)
        v = jnp.concatenate([v, jnp.ones((16, v.shape[1]), BF16)], axis=0)
        acc[group, blk] = acc[group, blk] * fade + mm(v, p)

    def mix(at, s_ref, x_ref):
        group, blk, step = at
        tiles = [
            held[step, size + DH * t:size + DH * (t + 1), :]
            for held, size in ((kva, SIZES[0]), (kvb, SIZES[1]))
            for t in range(size // DH)
        ]
        mix_in(group, blk, s_ref[0:OLD, :], x_ref, tiles)

    def mix_new(i, blk, s_ref, x_ref, first=0, count=GROUP):
        tiles = [nw[i * GROUP + j, NEW:2 * NEW, :] for j in range(first, first + count)]
        mix_in(0, blk, s_ref[0:count * NEW, :], x_ref, tiles)

    def kv_arrive(s):
        for d in range(2):
            kv_copy(d, s).wait_recv()
            if s <= 2:
                own_keys(d, s).wait_recv()
            if s + 2 < ZN:
                kv_copy(d, s + 2).start()

    def n_arrive(n):
        for d in range(2):
            n_copy(d, n).wait_recv()
            if n + 2 < ZN:
                n_copy(d, n + 2).start()

    def partials(group, b):
        blk, c = b // 2, (b % 2) * QB
        a = acc[group, blk, :, c:c + QB]
        total = a[DH:DH + 1]
        lse = top[group, blk, :, c:c + QB] + jnp.log(total) * LOG2E
        return a[:DH] / total, lse

    def finish(b):
        o, lse = partials(1, b)
        so[b, 0:DH, :] = o.astype(BF16)
        high = lse.astype(BF16).astype(F32)
        middle = (lse - high).astype(BF16).astype(F32)
        low = lse - high - middle
        row = lax.broadcasted_iota(jnp.int32, (16, QB), 0)
        so[b, DH:OROWS, :] = jnp.where(
            row == 0, high, jnp.where(row == 1, middle, low)
        ).astype(BF16)
        o_copy(b).start()

    def q_arrive(b):
        q_copy(b).wait_recv()

    def w_begin():
        w_copy.start()

    def n_begin():
        w_copy.wait_recv()
        for n in (1, 2):
            for d in range(2):
                n_copy(d, n).start()

    after = {
        0: [(kv_arrive, 1)],
        2: [(q_arrive, 0), (q_arrive, 1)],
        4: [(kv_arrive, 2)],
        7: [(kv_arrive, 3)],
        10: [(q_arrive, 2), (q_arrive, 3), (w_begin,)],
        11: [(kv_arrive, 4)],
        15: [(kv_arrive, 5), (n_begin,)],
        19: [(kv_arrive, 6)],
        22: [(kv_arrive, 7)],
        24: [(finish, 0), (finish, 1), (n_arrive, 1)],
        25: [(finish, 2), (finish, 3)],
        26: [(n_arrive, 2)],
        28: [(n_arrive, 3)],
    }

    def sync(u, odd):
        table = {at: actions for at, actions in after.items() if at % 2 == odd}

        @pl.when(functools.reduce(jnp.logical_or, [u == at for at in table]))
        def _():
            for at, actions in table.items():
                @pl.when(u == at)
                def _(actions=actions):
                    for action, *given in actions:
                        action(*given)

    score(UNITS[0], s0, x0)

    def body(i, now):
        u = 2 * i
        then = unit(u + 1)
        score(then, s1, x1)
        mix(now, s0, x0)
        sync(u, 0)
        now = unit(u + 2)
        score(now, s0, x0)
        mix(then, s1, x1)
        sync(u + 1, 1)
        return now

    first = tuple(jnp.int32(value) for value in UNITS[0])
    lax.fori_loop(0, len(UNITS) // 2 - 1, body, first)
    score(UNITS[-1], s1, x1)
    mix(UNITS[-2], s0, x0)
    n_arrive(4)
    score_new(0, 0, s0, x0)
    mix(UNITS[-1], s1, x1)

    def late(i, carry):
        score_new(i, 1, s1, x1)
        mix_new(i, 0, s0, x0)

        @pl.when(i == 0)
        def _():
            n_arrive(5)

        score_new(i + 1, 0, s0, x0)
        mix_new(i, 1, s1, x1)
        return carry

    def out_copy(b):
        return pltpu.make_async_copy(
            out_ref.at[:, pl.ds(b * QB, QB)], out_hbm.at[:, pl.ds(b * QB, QB)], out_sem.at[b]
        )

    def result(b):
        own, lse = partials(0, b)
        other = ro[b, 0:DH, :].astype(F32)
        rows = ro[b, DH:OROWS, :].astype(F32)
        lse_other = rows[0:1] + rows[1:2] + rows[2:3]
        largest = jnp.maximum(lse, lse_other)
        e_own, e_other = jnp.exp2(lse - largest), jnp.exp2(lse_other - largest)
        share = 1.0 / (e_own + e_other)
        mixed = own * (e_own * share) + other * (e_other * share)
        for h in range(QB // DH):
            c = b * QB + h * DH
            out_ref[:, c:c + DH] = mixed[:, h * DH:(h + 1) * DH].T.astype(BF16)
        out_copy(b).start()

    lax.fori_loop(0, LATE - 2, late, 0)
    end, half = LATE - 1, GROUP // 2
    score_new(end - 1, 1, s1, x1)
    mix_new(end - 1, 0, s0, x0)
    n_arrive(6)
    score_new(end, 0, s0, x0, 0, half)
    mix_new(end - 1, 1, s1, x1)
    score_new(end, 1, s1, x1, 0, half)
    mix_new(end, 0, s0, x0, 0, half)
    n_arrive(7)
    score_new(end, 0, s0, x0, half, half)
    mix_new(end, 1, s1, x1, 0, half)
    score_new(end, 1, s1, x1, half, half)
    mix_new(end, 0, s0, x0, half, half)
    for b in (0, 1):
        o_copy(b).wait_recv()
    mix_new(end, 1, s1, x1, half, half)
    result(0)
    result(1)
    for b in (2, 3):
        o_copy(b).wait_recv()
        result(b)

    for d in range(2):
        for s in range(1, ZN):
            kv_copy(d, s).wait_send()
            if s <= 2:
                own_keys(d, s).wait_send()
            n_copy(d, s).wait_send()
    w_copy.wait_send()
    for b in range(NQB):
        out_copy(b).wait()
    for b in range(NQB):
        q_copy(b).wait_send()
        o_copy(b).wait_send()


def solution(mesh):
    freqs = 500000.0 ** (-(2.0 * np.arange(HALF, dtype=np.float64)) / DH)
    table = np.zeros((HALF, DH), np.float32)
    table[:, :HALF] = freqs[:, None]

    def part(q_new, k_new, v_new, k_cache, v_cache, new_pos):
        dma = pltpu.SemaphoreType.DMA
        return pl.pallas_call(
            kernel,
            out_shape=jax.ShapeDtypeStruct(q_new.shape, BF16),
            in_specs=[pl.BlockSpec(memory_space=pltpu.HBM)] * 7,
            out_specs=pl.BlockSpec(memory_space=pltpu.HBM),
            scratch_shapes=[
                pltpu.VMEM((Q_ROWS, NQB * QB), BF16),
                dma((NQB,)),
                pltpu.VMEM((Q_ROWS, NQB * QB), BF16),
                pltpu.VMEM((NEW, DH), BF16),
                pltpu.VMEM((NEW, DH), BF16),
                pltpu.VMEM((OLD, DH), BF16),
                pltpu.VMEM((1, Q_ROWS), jnp.int32),
                pltpu.VMEM((HALF, DH), F32),
                dma((7 + NQB,)),
                pltpu.VMEM((2, NQB, DH, QB), BF16),
                pltpu.VMEM((ZN, 2 * SIZES[0], DH), BF16),
                pltpu.VMEM((ZN, 2 * SIZES[1], DH), BF16),
                pltpu.VMEM((2 * ZN, ROWS, DH), BF16),
                pltpu.VMEM((8, DH), F32),
                pltpu.VMEM((2, NCB, OROWS, CB), F32),
                pltpu.VMEM((2, NCB, 1, CB), F32),
                pltpu.VMEM((OLD, CB), F32),
                pltpu.VMEM((OLD, CB), F32),
                pltpu.VMEM((1, CB), F32),
                pltpu.VMEM((1, CB), F32),
                pltpu.VMEM((NQB, OROWS, QB), BF16),
                pltpu.VMEM((NQB, OROWS, QB), BF16),
                dma((2, 2)), dma((2, 2)),
                dma((2, ZN - 1)), dma((2, ZN - 1)),
                dma((2, ZN - 1)), dma((2, ZN - 1)),
                dma((NQB,)), dma((NQB,)), dma((NQB,)), dma((NQB,)),
                dma, dma,
            ],
            compiler_params=pltpu.CompilerParams(
                collective_id=0, has_side_effects=True, vmem_limit_bytes=64 << 20
            ),
        )(q_new, k_new, v_new, k_cache, v_cache, new_pos.reshape(1, -1), jnp.asarray(table))

    rows = P(("rep", "ctx"), "head")
    return jax.shard_map(
        part,
        mesh=mesh,
        in_specs=(rows,) * 5 + (P(("rep", "ctx")),),
        out_specs=rows,
        check_vma=False,
    )
```
